128 devices in a mesh: pts: 16 (over z, y), feat: 8 (over x, core).
Axes of the slice: x: 4, y: 4, z: 4, core: 2. Of those that a mesh axis runs over, the one named last changes fastest.
Arguments:
- points_x: float32 [3, 131072], P(None, 'pts'), may hold values from -2 to 2
- emb_x: bfloat16 [64, 131072], P(None, 'pts'), may hold values from -0.75 to 0.75
- points_y: float32 [3, 131072], P(None, 'pts'), may hold values from -2 to 2
- emb_y: bfloat16 [64, 131072], P(None, 'pts'), may hold values from -0.75 to 0.75
- mass_x: float32 [131072], P('pts'), may hold values from 0.25 to 4
- mass_y: float32 [131072], P('pts'), may hold values from 0.25 to 4
- grad_u: float32 [131072], P('pts'), may hold values from -6 to 6
- grad_v: float32 [131072], P('pts'), may hold values from -6 to 6
- omega_coord: float32 [3, 2048], P(None, 'feat'), may hold values from -4 to 4
- omega_emb: bfloat16 [64, 2048], P(None, 'feat'), may hold values from -4 to 4
Outputs:
- grad_emb_x: float32 [64, 131072], P(None, 'pts')
- grad_emb_y: float32 [64, 131072], P(None, 'pts')
The draws below stay inside these ranges and needn't reach their ends.
All inputs are finite; a program needn't handle non-finite values.
Results may differ from the reference program's by a relative error of at most 0.0003.
Values may be sent and summed in bfloat16 or wider, within the bound.
A program may use at most 192 MiB of HBM per device.

```python
import jax
import jax.numpy as jnp
from jax import lax

R = 2048
EMB = 64
PTS_DEV = 8192
ITERS = 3
NPTS = 131072


def block_signs(key, stream):
    key = jax.random.fold_in(key, stream)
    blocks = NPTS // PTS_DEV
    ranking = jax.random.permutation(jax.random.fold_in(key, 1), blocks)
    major_sign = jnp.where(ranking % 2 == 0, 1.0, -1.0).astype(jnp.float32)
    coin_flips = jax.random.randint(jax.random.fold_in(key, 2), (blocks,), 0, 2)
    minor_sign = jnp.where(coin_flips == 0, 1.0, -1.0).astype(jnp.float32)
    return (jnp.repeat(major_sign, PTS_DEV, total_repeat_length=NPTS), jnp.repeat(minor_sign, PTS_DEV, total_repeat_length=NPTS))


def place_points(major_sign, minor_sign, jitter, centre_major, centre_minor):
    major_axis = centre_major * major_sign + 0.15 * jitter[0]
    minor_axis = centre_minor * minor_sign + 0.15 * jitter[1]
    depth_axis = 0.3 * jitter[2]
    return jnp.clip(jnp.stack([major_axis, minor_axis, depth_axis]), -2.0, 2.0)


def draw_points_x(key, part):
    major_sign, minor_sign = block_signs(key, 1)
    key = jax.random.fold_in(key, 11)
    jitter = jax.random.normal(key, (3, NPTS), jnp.float32)
    return place_points(major_sign, minor_sign, jitter, 1.5, 0.8)


def draw_points_y(key, part):
    major_sign, minor_sign = block_signs(key, 2)
    key = jax.random.fold_in(key, 12)
    jitter = jax.random.normal(key, (3, NPTS), jnp.float32)
    return place_points(major_sign, minor_sign, jitter, 1.5, 0.8)


def draw_mass_x(key, part):
    major_sign, minor_sign = block_signs(key, 1)
    key = jax.random.fold_in(key, 13)
    jitter = jnp.clip(0.25 * jax.random.normal(key, (NPTS,), jnp.float32), -0.45, 0.45)
    return jnp.clip(jnp.exp(0.55 * major_sign + 0.3 * minor_sign + jitter), 0.25, 4.0)


def draw_mass_y(key, part):
    major_sign, minor_sign = block_signs(key, 2)
    key = jax.random.fold_in(key, 14)
    jitter = jnp.clip(0.25 * jax.random.normal(key, (NPTS,), jnp.float32), -0.45, 0.45)
    return jnp.clip(jnp.exp(-0.55 * major_sign + 0.3 * minor_sign + jitter), 0.25, 4.0)


def draw_grad_u(key, part):
    signs = block_signs(key, 1)
    key = jax.random.fold_in(key, 15)
    jitter = jax.random.normal(key, (NPTS,), jnp.float32)
    return jnp.clip(0.8 * signs[1] + 0.6 * jitter, -6.0, 6.0)


def draw_grad_v(key, part):
    signs = block_signs(key, 2)
    key = jax.random.fold_in(key, 16)
    jitter = jax.random.normal(key, (NPTS,), jnp.float32)
    return jnp.clip(0.8 * signs[0] + 0.6 * jitter, -6.0, 6.0)


def block_scale(key, shape, pieces, smallest, largest):
    gain = 1.0
    for axis_at, shards_of in pieces:
        heights = jax.random.uniform(jax.random.fold_in(jax.random.fold_in(key, 6), axis_at), (shards_of,), jnp.float32, smallest / len(pieces), largest / len(pieces))
        gain = gain * jnp.repeat(jnp.exp(heights), shape[axis_at] // shards_of).reshape((-1,) + (1,) * (len(shape) - 1 - axis_at))
    return gain


def normal_values(stream_key, extent, deviation, most, pieces=(), held_as=jnp.bfloat16):
    factor_of = block_scale(stream_key, extent, pieces, -0.22, 0.18) if pieces else 1.0
    entries = jax.random.normal(stream_key, extent, jnp.float32) * deviation * factor_of
    return jnp.minimum(jnp.maximum(entries, -most), most).astype(held_as)


def setup_inputs(seed: int = 0) -> dict:
    streams_of = jax.random.split(jax.random.key(seed), 11)
    return {
        "points_x": draw_points_x(jax.random.fold_in(streams_of[10], 71), 0),
        "emb_x": normal_values(streams_of[1], (EMB, NPTS), 0.125, 0.75, ((1, 16),)),
        "points_y": draw_points_y(jax.random.fold_in(streams_of[10], 71), 0),
        "emb_y": normal_values(streams_of[3], (EMB, NPTS), 0.125, 0.75, ((1, 16),)),
        "mass_x": draw_mass_x(jax.random.fold_in(streams_of[10], 71), 0),
        "mass_y": draw_mass_y(jax.random.fold_in(streams_of[10], 71), 0),
        "grad_u": draw_grad_u(jax.random.fold_in(streams_of[10], 71), 0),
        "grad_v": draw_grad_v(jax.random.fold_in(streams_of[10], 71), 0),
        "omega_coord": normal_values(streams_of[8], (3, R), 1.0, 4.0, ((1, 8),), jnp.float32),
        "omega_emb": normal_values(streams_of[9], (EMB, R), 1.0, 4.0, ((1, 8),)),
    }


highest = lax.Precision.HIGHEST

def feature_map(points, embedding, coord_seed, emb_seed):
    linear = lax.dot_general(emb_seed, embedding, (((0,), (0,)), ((), ())), preferred_element_type=jnp.float32)
    linear = linear + lax.dot_general(coord_seed, points, (((0,), (0,)), ((), ())), precision=highest, preferred_element_type=jnp.float32)
    emb_wide = embedding.astype(jnp.float32)
    half_norm = 0.5 * (lax.optimization_barrier(jnp.sum(points * points, axis=0)) + lax.optimization_barrier(jnp.sum(emb_wide * emb_wide, axis=0)))
    return jnp.exp(linear - half_norm[None, :])

def emb_gradient(feats, rows, cols, emb_seed, embedding):
    block = min(R, 256)

    def one_block(carry, index):
        start = (index * block).astype(jnp.int32)
        piece = lax.dynamic_slice_in_dim(feats, start, block, 0)
        weights = lax.dynamic_slice_in_dim(rows, start, block, 1)
        seeds = lax.dynamic_slice_in_dim(emb_seed, start, block, 1).astype(jnp.float32)
        bar_s = lax.dot_general(weights, cols, (((0,), (0,)), ((), ())), precision=highest, preferred_element_type=jnp.float32) * piece
        total, row_sum = carry
        total = total + jnp.dot(seeds, bar_s, precision=highest)
        return ((total, row_sum + lax.optimization_barrier(jnp.sum(bar_s, axis=0))), None)
    init = (jnp.zeros((embedding.shape[0], feats.shape[1]), jnp.float32), jnp.zeros((feats.shape[1],), jnp.float32))
    (total, row_sum), _ = lax.scan(one_block, init, jnp.arange(R // block, dtype=jnp.int32))
    return total - embedding.astype(jnp.float32) * row_sum[None, :]

def reference(points_x, emb_x, points_y, emb_y, mass_x, mass_y, grad_u, grad_v, omega_coord, omega_emb):
    feat_x = feature_map(points_x, emb_x, omega_coord, omega_emb)
    feat_y = feature_map(points_y, emb_y, omega_coord, omega_emb)
    scaling = 1.0 / (R * NPTS)
    dual_v = jnp.ones((NPTS,), jnp.float32)
    saved = []
    for step in range(ITERS):
        col_c = jnp.dot(feat_y, dual_v, precision=highest)
        kern_v = scaling * jnp.dot(col_c, feat_x, precision=highest)
        dual_u = jnp.sqrt(mass_x / kern_v)
        col_d = jnp.dot(feat_x, dual_u, precision=highest)
        kern_u = scaling * jnp.dot(col_d, feat_y, precision=highest)
        new_v = jnp.sqrt(mass_y / kern_u)
        saved.append((dual_v, col_c, kern_v, dual_u, col_d, kern_u, new_v))
        dual_v = new_v
    back_v = grad_v
    x_rows, x_cols, y_rows, y_cols = ([], [], [], [])
    for step in reversed(range(ITERS)):
        prev_v, col_c, kern_v, dual_u, col_d, kern_u, new_v = saved[step]
        back_ku = -0.5 * new_v * back_v / kern_u
        back_d = scaling * jnp.dot(feat_y, back_ku, precision=highest)
        back_u = jnp.dot(back_d, feat_x, precision=highest)
        if step == ITERS - 1:
            back_u = back_u + grad_u
        reverse_kernel_value = -0.5 * dual_u * back_u / kern_v
        back_c = scaling * jnp.dot(feat_x, reverse_kernel_value, precision=highest)
        if step > 0:
            back_v = jnp.dot(back_c, feat_y, precision=highest)
        x_rows += [back_d, scaling * col_c]
        x_cols += [dual_u, reverse_kernel_value]
        y_rows += [scaling * col_d, back_c]
        y_cols += [back_ku, prev_v]
    grad_x = emb_gradient(feat_x, jnp.stack(x_rows), jnp.stack(x_cols), omega_emb, emb_x)
    grad_y = emb_gradient(feat_y, jnp.stack(y_rows), jnp.stack(y_cols), omega_emb, emb_y)
    return (grad_x, grad_y)
```

```python
import jax
import jax.numpy as jnp
from jax import lax
from jax.experimental import pallas as pl
from jax.experimental.pallas import tpu as pltpu
from jax.sharding import PartitionSpec as P

MESH = pl.DeviceIdType.MESH
F32, BF16 = jnp.float32, jnp.bfloat16
SCALING = 1.0 / 268435456
STEPS = 3
PTS = 2048
FEATS = 1024
ROUNDS = 4 * STEPS
HALF = PTS // 2


def hop(k):
    return min(k, 4 - k)


OFFSETS = sorted(
    ((a, b, d) for a in range(4) for b in range(4) for d in range(4) if a or b or d),
    key=lambda o: -(hop(o[0]) + hop(o[1]) + hop(o[2])),
)
PEERS = len(OFFSETS)


def split3(v):
    one = v.astype(BF16).astype(F32)
    rest = v - one
    two = rest.astype(BF16).astype(F32)
    return one, two, (rest - two).astype(BF16).astype(F32)


def split2(v):
    one = v.astype(BF16)
    return one, (v - one.astype(F32)).astype(BF16)


def tree(terms):
    terms = list(terms)
    while len(terms) > 1:
        terms = [
            terms[i] + terms[i + 1] if i + 1 < len(terms) else terms[i]
            for i in range(0, len(terms), 2)
        ]
    return terms[0]


def kernel(
    points_x, emb_x, points_y, emb_y, mass_x, mass_y, grad_u, grad_v, coord, seeds,
    out_x, out_y,
    feat_x, feat_y, pts_in, emb_in, vec_in, om_c, om_e, om_ext, om_stage, om_t, xs_stage, xs_x, xs_y,
    acc, cb, send, buf, ksend, krecv, rows_c, rows_d, rows_bd, rows_bc,
    col_u, col_v, col_kv, col_ku, col_bku, col_bkv, terms_a, terms_b, total_x, total_y,
    gsend, grecv, own,
    in_sem, om_send, om_recv, send_sem, recv_sem, k_send, k_recv, g_send, g_recv,
    o_local, o_send, o_recv, f_send, f_recv,
):
    p, f = lax.axis_index("pts"), lax.axis_index("feat")
    z, y, x, c = p // 4, p % 4, f // 2, f % 2
    sibling = (p, x * 2 + (1 - c))
    planes = [[((z + a) % 4) * 4 + (y + b) % 4 for b in range(4)] for a in range(4)]
    along = [((x + d) % 4) * 2 + c for d in range(4)]
    chips = [(planes[a][b], along[d]) for a, b, d in OFFSETS]
    ring = [(p, along[d]) for d in (2, 1, 3)]

    barrier = pltpu.get_barrier_semaphore()
    for device in chips + [sibling]:
        pl.semaphore_signal(barrier, inc=1, device_id=device, device_id_type=MESH)

    lanes = pl.ds(pl.multiple_of(x * PTS, PTS), PTS)
    rows16 = pl.ds(pl.multiple_of(x * 16, 16), 16)
    loads = [
        pltpu.make_async_copy(points_x.at[:, lanes], pts_in.at[0], in_sem.at[0]),
        pltpu.make_async_copy(points_y.at[:, lanes], pts_in.at[1], in_sem.at[1]),
        pltpu.make_async_copy(emb_x.at[:, lanes], emb_in.at[0], in_sem.at[2]),
        pltpu.make_async_copy(emb_y.at[:, lanes], emb_in.at[1], in_sem.at[3]),
    ] + [
        pltpu.make_async_copy(ref.at[rows16, :], vec_in.at[i], in_sem.at[4 + i])
        for i, ref in enumerate((mass_x, mass_y, grad_u, grad_v))
    ]
    for load in loads:
        load.start()

    total_x[...] = jnp.zeros_like(total_x)
    total_y[...] = jnp.zeros_like(total_y)
    om_stage[...] = jnp.zeros_like(om_stage)
    xs_stage[...] = jnp.zeros_like(xs_stage)
    terms_a[...] = jnp.zeros_like(terms_a)
    terms_b[...] = jnp.zeros_like(terms_b)
    om_ext[...] = jnp.zeros_like(om_ext)
    rows_bc[STEPS + 1] = jnp.zeros((8, 128), F32)
    col_v[0] = jnp.ones((16, 128), F32)
    for load in loads:
        load.wait()

    for which, ref in ((0, xs_x), (1, xs_y)):
        pts = pts_in[which]
        wide = emb_in[which].astype(F32)
        half = 0.5 * (
            jnp.sum(pts * pts, axis=0, keepdims=True)
            + jnp.sum(wide * wide, axis=0, keepdims=True)
        )
        p1, p2, p3 = split3(pts)
        for i, part in enumerate((p1, p2, p3, p1, p2, p1)):
            xs_stage[3 * i : 3 * i + 3, :] = part
        for i, part in enumerate(split3(-half)):
            xs_stage[18 + i : 19 + i, :] = part
        ref[0:64, :] = emb_in[which]
        ref[64:128, :] = xs_stage[...].astype(BF16)

    pl.semaphore_wait(barrier, PEERS + 1)
    om_e[x] = seeds[...]
    om_c[x] = coord[...]
    om_copies = []
    for i, device in enumerate(ring):
        for k, ref in enumerate((om_e, om_c)):
            copy = pltpu.make_async_remote_copy(
                src_ref=ref.at[x], dst_ref=ref.at[x], send_sem=om_send.at[k, i],
                recv_sem=om_recv.at[k], device_id=device, device_id_type=MESH,
            )
            copy.start()
            om_copies.append(copy)
    for k, ref in enumerate((om_e, om_c)):
        three = ref.at[pl.ds(0, 3)]
        pltpu.make_async_copy(three, three, om_recv.at[k]).wait()
    for copy in om_copies:
        copy.wait_send()
    for s in range(4):
        om_stage[0:64, :] = om_e[s].astype(F32)
        o1, o2, o3 = split3(om_c[s])
        for i, part in enumerate((o1, o1, o1, o2, o2, o3)):
            om_stage[64 + 3 * i : 67 + 3 * i, :] = part
        om_stage[82:85, :] = jnp.ones((3, 256), F32)
        om_t[s * 256 : (s + 1) * 256, :] = om_stage[...].T.astype(BF16)
        om_ext[0:64, s * 256 : (s + 1) * 256] = om_e[s]
    om_ext[64:80, :] = jnp.where(
        lax.broadcasted_iota(jnp.int32, (16, FEATS), 0) == 0, 1.0, 0.0
    ).astype(BF16)

    def build(feat, xs):
        def block(i, _):
            r = pl.ds(pl.multiple_of((i // 4) * 256, 256), 256)
            l = pl.ds(pl.multiple_of((i % 4) * 512, 512), 512)
            feat[r, l] = jnp.exp(jnp.dot(om_t[r, :], xs[:, l], preferred_element_type=F32))
            return 0

        lax.fori_loop(0, 16, block, 0)

    row_at = lax.broadcasted_iota(jnp.int32, (8, 128), 0)

    def round_start(r):
        ones = jnp.ones((8, 128), BF16)
        parts = [
            lax.dot_general(
                ones, part.astype(BF16), (((1,), (1,)), ((), ())), preferred_element_type=F32
            )
            for part in split3(acc[...])
        ]
        flat = parts[0] + (parts[1] + parts[2])
        own_sum = flat[:, 0:128]
        for a in range(1, 8):
            own_sum = jnp.where(row_at == a, flat[:, a * 128 : (a + 1) * 128], own_sum)
        send[r] = own_sum
        for k, device in enumerate(chips):
            pltpu.make_async_remote_copy(
                src_ref=send.at[r], dst_ref=buf.at[r, k], send_sem=send_sem.at[r],
                recv_sem=recv_sem.at[r], device_id=device, device_id_type=MESH,
            ).start()

    def round_wait(r):
        pltpu.make_async_copy(buf.at[r], buf.at[r], recv_sem.at[r]).wait()
        return tree([send[r]] + [buf[r, k] for k in range(PEERS)])

    def spread(value):
        turned = value.T
        for a in range(8):
            cb[a * 128 : (a + 1) * 128, :] = jnp.broadcast_to(turned[:, a : a + 1], (128, 128))

    def over_features(feat, r):
        for h in range(2):

            def block(i, sums):
                sums = list(sums)
                for k in range(8):
                    rows = pl.ds(pl.multiple_of(i * 64, 64) + 8 * k, 8)
                    weight = cb[rows, :]
                    for j in range(8):
                        at = h * HALF + j * 128
                        sums[j] = sums[j] + feat[rows, at : at + 128] * weight
                return tuple(sums)

            sums = lax.fori_loop(
                0, FEATS // 64, block, tuple(jnp.zeros((8, 128), F32) for _ in range(8))
            )
            for j in range(8):
                ksend[r, h, j : j + 1, :] = jnp.sum(sums[j], axis=0, keepdims=True)
            pltpu.make_async_remote_copy(
                src_ref=ksend.at[r, h], dst_ref=krecv.at[r, h], send_sem=k_send.at[r, h],
                recv_sem=k_recv.at[r, h], device_id=sibling, device_id_type=MESH,
            ).start()

    def over_points(feat, h, weights):
        spreads = [jnp.broadcast_to(weights[j : j + 1, :], (8, 128)) for j in range(8)]

        def block(i, _):
            for k in range(8):
                rows = pl.ds(pl.multiple_of(i * 64, 64) + 8 * k, 8)
                part = tree(
                    feat[rows, h * HALF + j * 128 : h * HALF + (j + 1) * 128] * spreads[j]
                    for j in range(8)
                )
                acc[rows, :] = part if h == 0 else acc[rows, :] + part
            return 0

        lax.fori_loop(0, FEATS // 64, block, 0)

    def half_step(feat, r, update):
        over_features(feat, r)
        for h in range(2):
            pltpu.make_async_copy(krecv.at[r, h], krecv.at[r, h], k_recv.at[r, h]).wait()
            over_points(feat, h, update(pl.ds(h * 8, 8), ksend[r, h] + krecv[r, h]))

    def add_terms(feat, total, pairs):
        for i, (row, col) in enumerate(pairs):
            r1, r2 = (v.astype(F32) for v in split2(row))
            c1, c2 = (v.astype(F32) for v in split2(col))
            for k, (left, right) in enumerate(((r1, c1), (r1, c2), (r2, c1))):
                at = 3 * i + k
                for a in range(8):
                    terms_a[at : at + 1, a * 128 : (a + 1) * 128] = left[a : a + 1, :]
                for a in range(16):
                    terms_b[at : at + 1, a * 128 : (a + 1) * 128] = right[a : a + 1, :]

        def block(i, _):
            r = pl.ds(pl.multiple_of((i % 4) * 256, 256), 256)
            l = pl.ds(pl.multiple_of((i // 4) * 512, 512), 512)
            weight = lax.dot_general(
                terms_a[:, r].astype(BF16), terms_b[:, l].astype(BF16),
                (((0,), (0,)), ((), ())), preferred_element_type=F32,
            )
            hi, lo = split2(feat[r, l] * weight)
            left = om_ext[:, r]
            total[:, l] += jnp.dot(left, hi, preferred_element_type=F32) + jnp.dot(
                left, lo, preferred_element_type=F32
            )
            return 0

        lax.fori_loop(0, 16, block, 0)

    def finish(which, total):
        wide = emb_in[which].astype(F32)
        share = total[0:64, :] - wide * total[64:65, :]
        first, second = share[:, :HALF], share[:, HALF:]
        own[which] = jnp.where(c == 0, first, second)
        gsend[which] = jnp.where(c == 0, second, first)
        pltpu.make_async_remote_copy(
            src_ref=gsend.at[which], dst_ref=grecv.at[which], send_sem=g_send.at[which],
            recv_sem=g_recv.at[which], device_id=sibling, device_id_type=MESH,
        ).start()

    def place(which, out):
        pltpu.make_async_copy(grecv.at[which], grecv.at[which], g_recv.at[which]).wait()
        own[which] = own[which] + grecv[which]
        mine = out.at[:, pl.ds(pl.multiple_of(x * PTS + c * HALF, HALF), HALF)]
        for k, device in enumerate(ring + [sibling]):
            pltpu.make_async_remote_copy(
                src_ref=own.at[which], dst_ref=mine, send_sem=o_send.at[which, k],
                recv_sem=o_recv.at[which, k], device_id=device, device_id_type=MESH,
            ).start()
        pltpu.make_async_copy(own.at[which], mine, o_local.at[which]).start()

    def theirs(out, d, core):
        return out.at[:, pl.ds(pl.multiple_of(((x + 4 - d) % 4) * PTS + core * HALF, HALF), HALF)]

    build(feat_y, xs_y)
    for h in range(2):
        over_points(feat_y, h, jnp.ones((8, 128), F32))
    round_start(0)
    build(feat_x, xs_x)

    def forward(i, _):
        t = i + 1
        value = round_wait(2 * i)
        rows_c[t] = SCALING * value
        spread(value)

        def update_u(at, sums):
            kern = SCALING * sums
            dual = jnp.sqrt(vec_in[0, at, :] / kern)
            col_kv[t, at, :] = kern
            col_u[t, at, :] = dual
            return dual

        half_step(feat_x, 2 * i, update_u)
        round_start(2 * i + 1)
        value = round_wait(2 * i + 1)
        rows_d[t] = SCALING * value
        spread(value)

        def update_v(at, sums):
            kern = SCALING * sums
            dual = jnp.sqrt(vec_in[1, at, :] / kern)
            back = -0.5 * dual * vec_in[3, at, :] / kern
            col_ku[t, at, :] = kern
            col_v[t, at, :] = dual
            col_bku[t, at, :] = back
            return jnp.where(t == STEPS, back, dual)

        half_step(feat_y, 2 * i + 1, update_v)
        round_start(2 * i + 2)
        return 0

    lax.fori_loop(0, STEPS, forward, 0)

    def backward_x(j):
        t = STEPS - j
        r = 2 * STEPS + 2 * j
        add_terms(feat_y, total_y, ((rows_d[t], col_bku[t]), (rows_bc[t + 1], col_v[t])))
        value = SCALING * round_wait(r)
        rows_bd[t] = value
        spread(value)

        def update(at, sums):
            back_u = sums + jnp.where(t == STEPS, vec_in[2, at, :], 0.0)
            back = -0.5 * col_u[t, at, :] * back_u / col_kv[t, at, :]
            col_bkv[t, at, :] = back
            return back

        half_step(feat_x, r, update)
        round_start(r + 1)
        add_terms(feat_x, total_x, ((rows_bd[t], col_u[t]), (rows_c[t], col_bkv[t])))

    def backward(j, _):
        t = STEPS - j
        r = 2 * STEPS + 2 * j + 1
        backward_x(j)
        value = SCALING * round_wait(r)
        rows_bc[t] = value
        spread(value)

        def update(at, sums):
            back = -0.5 * col_v[t - 1, at, :] * sums / col_ku[t - 1, at, :]
            col_bku[t - 1, at, :] = back
            return back

        half_step(feat_y, r, update)
        round_start(r + 1)
        return 0

    lax.fori_loop(0, STEPS - 1, backward, 0)
    backward_x(STEPS - 1)
    finish(0, total_x)
    place(0, out_x)
    value = SCALING * round_wait(ROUNDS - 1)
    zero = jnp.zeros((16, 128), F32)
    add_terms(feat_y, total_y, ((value, col_v[0]), (jnp.zeros((8, 128), F32), zero)))
    finish(1, total_y)
    place(1, out_y)

    for which, out in ((0, out_x), (1, out_y)):
        for k, d in enumerate((2, 1, 3)):
            block = theirs(out, d, c)
            pltpu.make_async_copy(block, block, o_recv.at[which, k]).wait()
            pltpu.make_async_remote_copy(
                src_ref=block, dst_ref=block, send_sem=f_send.at[which, k],
                recv_sem=f_recv.at[which, k], device_id=sibling, device_id_type=MESH,
            ).start()
    for which, out in ((0, out_x), (1, out_y)):
        pltpu.make_async_copy(own.at[which], theirs(out, 0, c), o_local.at[which]).wait()
        other = theirs(out, 0, 1 - c)
        pltpu.make_async_copy(other, other, o_recv.at[which, 3]).wait()
        for k, d in enumerate((2, 1, 3)):
            other = theirs(out, d, 1 - c)
            pltpu.make_async_copy(other, other, f_recv.at[which, k]).wait()
            block = theirs(out, d, c)
            pltpu.make_async_copy(block, block, f_send.at[which, k]).wait()
        for k in range(4):
            pltpu.make_async_copy(own.at[which], own.at[which], o_send.at[which, k]).wait()
        pltpu.make_async_copy(gsend.at[which], gsend.at[which], g_send.at[which]).wait()

    def drain(r, _):
        pltpu.make_async_copy(buf.at[r], buf.at[r], send_sem.at[r]).wait()
        return 0

    lax.fori_loop(0, ROUNDS, drain, 0)

    def drain_k(r, _):
        for h in range(2):
            pltpu.make_async_copy(ksend.at[r, h], ksend.at[r, h], k_send.at[r, h]).wait()
        return 0

    lax.fori_loop(0, ROUNDS - 1, drain_k, 0)


def per_device(
    points_x, emb_x, points_y, emb_y, mass_x, mass_y, grad_u, grad_v, omega_coord, omega_emb
):
    vectors = [v.reshape(64, 128) for v in (mass_x, mass_y, grad_u, grad_v)]
    hbm = pl.BlockSpec(memory_space=pl.ANY)
    vmem = pl.BlockSpec(memory_space=pltpu.VMEM)
    out = jax.ShapeDtypeStruct((64, 4 * PTS), F32)
    dma = pltpu.SemaphoreType.DMA
    scratch = [
        pltpu.VMEM((FEATS, PTS), F32), pltpu.VMEM((FEATS, PTS), F32),
        pltpu.VMEM((2, 3, PTS), F32), pltpu.VMEM((2, 64, PTS), BF16), pltpu.VMEM((4, 16, 128), F32),
        pltpu.VMEM((4, 3, 256), F32), pltpu.VMEM((4, 64, 256), BF16), pltpu.VMEM((80, FEATS), BF16),
        pltpu.VMEM((128, 256), F32), pltpu.VMEM((FEATS, 128), BF16), pltpu.VMEM((64, PTS), F32),
        pltpu.VMEM((128, PTS), BF16), pltpu.VMEM((128, PTS), BF16),
        pltpu.VMEM((FEATS, 128), F32), pltpu.VMEM((FEATS, 128), F32),
        pltpu.VMEM((ROUNDS, 8, 128), F32), pltpu.VMEM((ROUNDS, PEERS, 8, 128), F32),
        pltpu.VMEM((ROUNDS, 2, 8, 128), F32), pltpu.VMEM((ROUNDS, 2, 8, 128), F32),
    ] + [pltpu.VMEM((STEPS + 2, 8, 128), F32)] * 4 + [pltpu.VMEM((STEPS + 1, 16, 128), F32)] * 6 + [
        pltpu.VMEM((16, FEATS), F32), pltpu.VMEM((16, PTS), F32),
        pltpu.VMEM((80, PTS), F32), pltpu.VMEM((80, PTS), F32),
        pltpu.VMEM((2, 64, HALF), F32), pltpu.VMEM((2, 64, HALF), F32), pltpu.VMEM((2, 64, HALF), F32),
        dma((8,)), dma((2, 3)), dma((2,)), dma((ROUNDS,)), dma((ROUNDS,)), dma((ROUNDS, 2)), dma((ROUNDS, 2)),
        dma((2,)), dma((2,)), dma((2,)), dma((2, 4)), dma((2, 4)), dma((2, 3)), dma((2, 3)),
    ]
    return pl.pallas_call(
        kernel,
        out_shape=(out, out),
        in_specs=[hbm] * 8 + [vmem] * 2,
        out_specs=(hbm, hbm),
        scratch_shapes=scratch,
        compiler_params=pltpu.CompilerParams(
            collective_id=0, has_side_effects=True, vmem_limit_bytes=56 * 2**20
        ),
    )(points_x, emb_x, points_y, emb_y, *vectors, omega_coord, omega_emb)


def solution(mesh):
    in_specs = (
        P(None, "pts"),
        P(None, "pts"),
        P(None, "pts"),
        P(None, "pts"),
        P("pts"),
        P("pts"),
        P("pts"),
        P("pts"),
        P(None, "feat"),
        P(None, "feat"),
    )
    out_specs = (P(None, "pts"), P(None, "pts"))
    return jax.shard_map(
        per_device, mesh=mesh, in_specs=in_specs, out_specs=out_specs, check_vma=False
    )
```
